32 devices in a mesh: grp: 2 (over y), pair: 4 (over z), rng: 4 (over x, core).
Axes of the slice: x: 2, y: 2, z: 4, core: 2. Of those that a mesh axis runs over, the one named last changes fastest.
Arguments:
- integrals: bfloat16 [12288, 16384], P(('grp', 'pair'), 'rng'), parts along dimension 0, may hold values from -0.046875 to 0.046875
- coefficients: bfloat16 [8192, 16], P('grp'), parts along dimension 0, may hold values from -6 to 6
- ket_shells: int32 [512, 2], P(('grp', 'rng')), parts along dimension 0, may hold values from 0 to 511
- block_ids: int32 [192], P(('grp', 'pair')), parts along dimension 0, may hold values from -1 to 47, as said below
- pair_owner: int32 [256], replicated, may hold values from 0 to 255, each once
Outputs:
- half: float32 [512, 3072], P(('grp', 'pair', 'rng')), parts along dimension 0
The draws below stay inside these ranges and needn't reach their ends.
There are 2 independent parts, one for each index of `grp`. The reference program is written for one: setup_inputs(seed, part) draws one part's arguments, and reference() takes and returns one part's arrays. A program takes and returns all parts, laid end to end along the dimension named above; an argument that names none is the same for every part. Nothing has to cross between parts.
Inputs may be any that keep to these rules, and one draw needn't show every extreme that they name: `block_ids`: -1 marks an empty slot; each block 0 to 47 stands in exactly one slot; of the 24 slots of one index of pair, 24, 12 or 6 are filled (a quarter, a quarter and half of the indices in every aligned group of four, in an order drawn), at positions drawn.
All inputs are finite; a program needn't handle non-finite values.
Results may differ from the reference program's by a relative error of at most 0.0029.
Values sent between devices are 32-bit elements; how exact they have to be, the bound alone decides.
No kernel may reach another device: no remote copies, remote signals or barrier semaphores. Data moves between devices by JAX's collectives and lax.ppermute only.
A program may use at most 128 MiB of HBM per device.

```python
import jax
import jax.numpy as jnp

NBF = 4096
SHELL = 8
BLOCK_PAIRS = 64
NSHELL = 512
NOCC = 16
NIJ = 256
SLOTS = 24
KET_BLOCKS = 256
KETS = 16384
BRA_SLOTS = 96
BRA_ROWS = 6144
BLOCKS = 48


def draw_block_ids(key, part):
    key = jax.random.fold_in(key, 7)
    key_count, key_rank, key_label = jax.random.split(key, 3)
    devices = BRA_SLOTS // SLOTS
    quarter = SLOTS // 4
    pattern = jnp.array([4, 2, 1, 1], dtype=jnp.int32) * quarter
    counts = jnp.tile(pattern, devices // 4)
    counts = counts[jax.random.permutation(key_count, devices)]
    slot_rank = jax.vmap(lambda each: jax.random.permutation(each, SLOTS))(jax.random.split(key_rank, devices)).astype(jnp.int32)
    live_slots = (slot_rank < counts[:, None]).reshape(-1)
    position = jnp.cumsum(live_slots.astype(jnp.int32)) - 1
    labels = jax.random.permutation(key_label, BLOCKS).astype(jnp.int32)
    picked = labels[jnp.clip(position, 0, BLOCKS - 1)]
    return jnp.where(live_slots, picked, -1).astype(jnp.int32)


def place_ends(drawn, key, smallest, top_value):
    spot = [jax.random.randint(jax.random.fold_in(key, axis), (), 0, length) for axis, length in enumerate(drawn.shape)]
    main_axis = drawn.shape.index(max(drawn.shape))
    beside = spot[:main_axis] + [(spot[main_axis] + 1) % drawn.shape[main_axis]] + spot[main_axis + 1:]
    return drawn.at[tuple(spot)].set(smallest).at[tuple(beside)].set(top_value)


def shard_levels(stream_key, shape, cuts, smallest, top_value):
    loudness, own = 1.0, jax.random.fold_in(stream_key, 6)
    for axis_at, parts in cuts:
        draws = jnp.exp(jax.random.uniform(jax.random.fold_in(own, axis_at), (parts,), jnp.float32, smallest / len(cuts), top_value / len(cuts)))
        loudness = loudness * jnp.repeat(draws, shape[axis_at] // parts).reshape([-1 if axis == axis_at else 1 for axis in range(len(shape))])
    return loudness


def scatter_about(own_key, dims, spread, limit, cuts=(), kind=jnp.bfloat16):
    entries = jax.random.normal(own_key, dims, jnp.float32) * spread
    if len(cuts) > 0:
        entries = shard_levels(own_key, dims, cuts, -0.22, 0.18) * entries
    return jnp.clip(entries, min=-limit, max=limit).astype(kind)


def setup_inputs(seed: int = 0, part: int = 0) -> dict:
    keys = jax.random.split(jax.random.key(seed), 6)
    own_keys = jax.random.split(jax.random.fold_in(keys[5], part), 6)
    integrals = scatter_about(own_keys[0], (BRA_ROWS, KETS), KETS ** -0.5, 0.046875, ((0, 4), (1, 4)))
    coefficients = scatter_about(own_keys[1], (NBF, NOCC), 1.0, 6.0)
    ket_shells = place_ends(jax.random.randint(own_keys[2], (KET_BLOCKS, 2), 0, NSHELL), jax.random.fold_in(own_keys[2], 1), 0, NSHELL - 1).astype(jnp.int32)
    block_ids = draw_block_ids(jax.random.fold_in(jax.random.fold_in(keys[5], part), 71), part)
    pair_owner = jax.random.permutation(keys[4], NIJ).astype(jnp.int32)
    return {"integrals": integrals, "coefficients": coefficients, "ket_shells": ket_shells, "block_ids": block_ids, "pair_owner": pair_owner}


def reference(integrals, coefficients, ket_shells, block_ids, pair_owner):
    offsets = jnp.arange(SHELL, dtype=jnp.int32)
    coef_full = coefficients.astype(jnp.float32)
    lam_coef = coef_full[ket_shells[:, 0:1] * SHELL + offsets[None, :]]
    sig_coef = coef_full[ket_shells[:, 1:2] * SHELL + offsets[None, :]]
    coef_pairs = jnp.einsum("kli,ksj->klsij", lam_coef, sig_coef).reshape(KETS, NIJ).astype(jnp.bfloat16)
    half_rows = jnp.dot(integrals, coef_pairs, preferred_element_type=jnp.float32)
    half_rows = half_rows[:, pair_owner]
    targets = jnp.arange(BLOCKS, dtype=jnp.int32)
    slot_numbers = jnp.arange(BRA_SLOTS, dtype=jnp.int32)
    source = jnp.sum(jnp.where(block_ids[None, :] == targets[:, None], slot_numbers[None, :], 0), axis=1).astype(jnp.int32)
    placed = half_rows.reshape(BRA_SLOTS, BLOCK_PAIRS, NIJ)[source]
    return placed.reshape(BLOCKS * BLOCK_PAIRS, NIJ).T
```

```python
import functools
import jax
import jax.numpy as jnp
from jax import lax
from jax.experimental import pallas as pl
from jax.experimental.pallas import tpu as pltpu
from jax.sharding import PartitionSpec as P

SHELL = 8
BLOCK_PAIRS = 64
NOCC = 16
NIJ = 256
LANES = 128
ROWS = 256
MIB = 1 << 20


def bits(size):
    return size.bit_length() - 1


def half_rows_kernel(
    pairs, ranges, shells, owner, coef, integrals, keep, send, table, lam, sig, cols, held, sems
):
    row_blocks = held.shape[0]
    kets = cols.shape[0] // BLOCK_PAIRS

    def fetch(step):
        return pltpu.make_async_copy(
            integrals.at[pl.ds(step * ROWS, ROWS), :], held.at[step], sems.at[step]
        )

    for step in range(row_blocks):
        fetch(step).start()

    me_pair, me_range = lax.axis_index("pair"), lax.axis_index("rng")
    rows_each = NIJ // (pairs * ranges)
    place = lax.broadcasted_iota(jnp.int32, (NIJ, NIJ), 1)
    inner = place % rows_each
    far_pair = (place // rows_each) % pairs
    order = place // (rows_each * pairs)
    far_range = jnp.zeros_like(order)
    for bit in range(bits(ranges)):
        far_range = far_range + (((order >> (bits(ranges) - 1 - bit)) & 1) << bit)
    target = ((far_pair ^ me_pair) * ranges + (far_range ^ me_range)) * rows_each + inner
    moved = (lax.broadcasted_iota(jnp.int32, (NIJ, NIJ), 0) == target).astype(jnp.bfloat16)
    orbital = lax.broadcasted_iota(jnp.int32, (NOCC, NIJ), 0)
    first = (owner[...] // NOCC == orbital).astype(jnp.bfloat16)
    second = (owner[...] % NOCC == orbital).astype(jnp.bfloat16)
    first = jnp.dot(first, moved, preferred_element_type=jnp.float32).astype(jnp.bfloat16)
    second = jnp.dot(second, moved, preferred_element_type=jnp.float32).astype(jnp.bfloat16)

    table[...] = coef[...].astype(jnp.float32).T

    for k in range(kets):
        here = pl.ds(k * SHELL, SHELL)
        lam[here, :NOCC] = table[pl.ds(pl.multiple_of(shells[0, k] * SHELL, SHELL), SHELL), :]
        sig[here, :NOCC] = table[pl.ds(pl.multiple_of(shells[1, k] * SHELL, SHELL), SHELL), :]
    lam[...] = jnp.dot(
        lam[:, :NOCC].astype(jnp.bfloat16), first, preferred_element_type=jnp.float32
    )
    sig[...] = jnp.dot(
        sig[:, :NOCC].astype(jnp.bfloat16), second, preferred_element_type=jnp.float32
    )
    for k in range(kets):
        here = pl.ds(k * SHELL, SHELL)
        both = lam[here, :][:, None, :] * sig[here, :][None, :, :]
        cols[pl.ds(k * BLOCK_PAIRS, BLOCK_PAIRS), :] = both.reshape(BLOCK_PAIRS, NIJ).astype(
            jnp.bfloat16
        )

    for step in range(row_blocks):
        fetch(step).wait()
        rows = jnp.dot(held[step], cols[...], preferred_element_type=jnp.float32).T
        here = pl.ds(step * ROWS, ROWS)
        keep[:, here] = rows[: NIJ // 2]
        send[:, here] = rows[NIJ // 2 :]


def half_rows(integrals, coefficients, ket_shells, pair_owner, pairs, ranges):
    rows, depth = integrals.shape
    kets = ket_shells.shape[0]
    half = jax.ShapeDtypeStruct((NIJ // 2, rows), jnp.float32)
    vmem = pl.BlockSpec(memory_space=pltpu.VMEM)
    return pl.pallas_call(
        functools.partial(half_rows_kernel, pairs, ranges),
        out_shape=(half, half),
        in_specs=[
            pl.BlockSpec(memory_space=pltpu.SMEM),
            vmem,
            vmem,
            pl.BlockSpec(memory_space=pl.ANY),
        ],
        out_specs=(vmem, vmem),
        scratch_shapes=[
            pltpu.VMEM((coefficients.shape[0], NOCC), jnp.float32),
            pltpu.VMEM((kets * SHELL, NIJ), jnp.float32),
            pltpu.VMEM((kets * SHELL, NIJ), jnp.float32),
            pltpu.VMEM((depth, NIJ), jnp.bfloat16),
            pltpu.VMEM((rows // ROWS, ROWS, depth), jnp.bfloat16),
            pltpu.SemaphoreType.DMA((rows // ROWS,)),
        ],
        compiler_params=pltpu.CompilerParams(vmem_limit_bytes=40 * MIB),
    )(ket_shells.T, pair_owner.reshape(1, NIJ), coefficients.T, integrals)


def place_kernel(slots, *refs):
    *pieces, out, numbers, scalars, sem = refs
    width = slots * BLOCK_PAIRS
    for d, piece in enumerate(pieces):
        numbers[pl.ds(d, 1), :] = piece[0:1, width:].astype(jnp.int32)
    copy = pltpu.make_async_copy(numbers, scalars, sem)
    copy.start()
    copy.wait()
    lane = lax.broadcasted_iota(jnp.int32, (out.shape[0], LANES), 1)
    upper = lane // BLOCK_PAIRS
    for d, piece in enumerate(pieces):
        for slot in range(slots):
            block = scalars[d, slot]
            side = slot % 2

            @pl.when(block >= 0)
            def _():
                value = piece[:, pl.ds((slot // 2) * LANES, LANES)]
                value = jnp.where(
                    block % 2 == side, value, pltpu.roll(value, BLOCK_PAIRS, 1)
                )
                there = pl.ds(pl.multiple_of((block // 2) * LANES, LANES), LANES)
                out[:, there] = jnp.where(upper == block % 2, value, out[:, there])


def placed_rows(pieces, slots, blocks):
    rows = pieces[0].shape[0]
    vmem = pl.BlockSpec(memory_space=pltpu.VMEM)
    return pl.pallas_call(
        functools.partial(place_kernel, slots),
        out_shape=jax.ShapeDtypeStruct((rows, blocks * BLOCK_PAIRS), jnp.float32),
        in_specs=[vmem] * len(pieces),
        out_specs=vmem,
        scratch_shapes=[
            pltpu.VMEM((len(pieces), LANES), jnp.int32),
            pltpu.SMEM((len(pieces), LANES), jnp.int32),
            pltpu.SemaphoreType.DMA,
        ],
    )(*pieces)


def swap(value, axis, size, far):
    return lax.ppermute(value, axis, [(i, i ^ far) for i in range(size)])


def local(pairs, ranges, integrals, coefficients, ket_shells, block_ids, pair_owner):
    slots = block_ids.shape[0]
    keep, send = half_rows(integrals, coefficients, ket_shells, pair_owner, pairs, ranges)
    rows = keep + swap(send, "rng", ranges, 1)
    each = NIJ // (pairs * ranges)
    rows = rows.reshape(ranges // 2, pairs, each, rows.shape[1])
    numbers = jnp.pad(block_ids.astype(jnp.float32), (0, LANES - slots))
    numbers = jnp.broadcast_to(numbers, (each, LANES))
    step = max(pairs // 2, 1)
    far = list(range(step, pairs)) + list(range(step))[::-1]
    pieces = [None] * pairs
    for start in range(0, pairs, step):
        group = far[start : start + step]
        part = jnp.stack([rows[:, d] for d in group], 1)
        for bit in range(1, bits(ranges)):
            half = part.shape[0] // 2
            part = part[:half] + swap(
                part[half:].reshape(-1, part.shape[-1]), "rng", ranges, 1 << bit
            ).reshape(part[half:].shape)
        for at, d in enumerate(group):
            piece = jnp.concatenate([part[0, at], numbers], axis=1)
            pieces[d] = swap(piece, "pair", pairs, d) if d else piece
    return placed_rows(pieces, slots, slots * pairs // 2)


def solution(mesh):
    placed = (
        P(("grp", "pair"), "rng"),
        P("grp", None),
        P(("grp", "rng"), None),
        P(("grp", "pair")),
        P(),
    )
    return jax.shard_map(
        functools.partial(local, mesh.shape["pair"], mesh.shape["rng"]),
        mesh=mesh,
        in_specs=placed,
        out_specs=P(("grp", "pair", "rng"), None),
        check_vma=False,
    )
```

```python
import functools
import jax
import jax.numpy as jnp
from jax import lax
from jax.experimental import pallas as pl
from jax.experimental.pallas import tpu as pltpu
from jax.sharding import PartitionSpec as P

SHELL = 8
BLOCK_PAIRS = 64
NOCC = 16
NIJ = 256
LANES = 128
ROWS = 512
MIB = 1 << 20


def bits(size):
    return size.bit_length() - 1


def half_rows_kernel(
    pairs, ranges, shells_at, owner_at, coef_at, integrals, keep, send, shells, owner, coef,
    table, lam, sig, cols, held, small, sems,
):
    blocks = sems.shape[0]
    rows = held.shape[0] // blocks
    kets = cols.shape[0] // BLOCK_PAIRS

    def fetch(step):
        here = pl.ds(step * rows, rows)
        return pltpu.make_async_copy(integrals.at[here, :], held.at[here, :], sems.at[step])

    tables = [
        pltpu.make_async_copy(shells_at, shells, small.at[0]),
        pltpu.make_async_copy(owner_at, owner, small.at[1]),
        pltpu.make_async_copy(coef_at, coef, small.at[2]),
    ]
    for copy in tables:
        copy.start()
    for step in range(blocks):
        fetch(step).start()

    me_pair, me_range = lax.axis_index("pair"), lax.axis_index("rng")
    rows_each = NIJ // (pairs * ranges)
    place = lax.broadcasted_iota(jnp.int32, (SHELL, NIJ), 1)
    inner = place % rows_each
    far_pair = (place // rows_each) % pairs
    order = place // (rows_each * pairs)
    far_range = jnp.zeros_like(order)
    for bit in range(bits(ranges)):
        far_range = far_range + (((order >> (bits(ranges) - 1 - bit)) & 1) << bit)
    target = ((far_pair ^ me_pair) * ranges + (far_range ^ me_range)) * rows_each + inner
    moved = (lax.broadcasted_iota(jnp.int32, (NIJ, NIJ), 0) == target[0:1, :]).astype(jnp.bfloat16)
    orbital = lax.broadcasted_iota(jnp.int32, (NOCC, NIJ), 0)
    for copy in tables:
        copy.wait()
    picks = jnp.concatenate(
        [
            (owner[...] // NOCC == orbital).astype(jnp.bfloat16),
            (owner[...] % NOCC == orbital).astype(jnp.bfloat16),
        ],
        axis=0,
    )
    picks = jnp.dot(picks, moved, preferred_element_type=jnp.float32).astype(jnp.bfloat16)

    table[...] = coef[...].astype(jnp.float32).T

    for k in range(kets):
        here = pl.ds(k * SHELL, SHELL)
        lam[here, :NOCC] = table[pl.ds(pl.multiple_of(shells[0, k] * SHELL, SHELL), SHELL), :]
        sig[here, :NOCC] = table[pl.ds(pl.multiple_of(shells[1, k] * SHELL, SHELL), SHELL), :]
    lam[...] = jnp.dot(
        lam[:, :NOCC].astype(jnp.bfloat16), picks[:NOCC], preferred_element_type=jnp.float32
    )
    sig[...] = jnp.dot(
        sig[:, :NOCC].astype(jnp.bfloat16), picks[NOCC:], preferred_element_type=jnp.float32
    )
    for k in range(kets):
        here = pl.ds(k * SHELL, SHELL)
        both = lam[here, :][:, None, :] * sig[here, :][None, :, :]
        cols[pl.ds(k * BLOCK_PAIRS, BLOCK_PAIRS), :] = both.reshape(BLOCK_PAIRS, NIJ).astype(
            jnp.bfloat16
        )

    for step in range(blocks):
        fetch(step).wait()
        here = pl.ds(step * rows, rows)
        part = lax.dot_general(
            cols[...], held[here, :], (((0,), (1,)), ((), ())), preferred_element_type=jnp.float32
        )
        keep[:, here] = part[: NIJ // 2]
        send[:, here] = part[NIJ // 2 :]


def half_rows(integrals, coefficients, ket_shells, pair_owner, pairs, ranges):
    rows, depth = integrals.shape
    kets = ket_shells.shape[0]
    half = jax.ShapeDtypeStruct((NIJ // 2, rows), jnp.float32)
    vmem = pl.BlockSpec(memory_space=pltpu.VMEM)
    return pl.pallas_call(
        functools.partial(half_rows_kernel, pairs, ranges),
        out_shape=(half, half),
        in_specs=[pl.BlockSpec(memory_space=pl.ANY)] * 4,
        out_specs=(vmem, vmem),
        scratch_shapes=[
            pltpu.SMEM((2, kets), jnp.int32),
            pltpu.VMEM((1, NIJ), jnp.int32),
            pltpu.VMEM((NOCC, coefficients.shape[0]), jnp.bfloat16),
            pltpu.VMEM((coefficients.shape[0], NOCC), jnp.float32),
            pltpu.VMEM((kets * SHELL, NIJ), jnp.float32),
            pltpu.VMEM((kets * SHELL, NIJ), jnp.float32),
            pltpu.VMEM((depth, NIJ), jnp.bfloat16),
            pltpu.VMEM((rows, depth), jnp.bfloat16),
            pltpu.SemaphoreType.DMA((3,)),
            pltpu.SemaphoreType.DMA((rows // ROWS,)),
        ],
        compiler_params=pltpu.CompilerParams(vmem_limit_bytes=52 * MIB),
    )(ket_shells.T, pair_owner.reshape(1, NIJ), coefficients.T, integrals)


def place_kernel(slots, *refs):
    *pieces, out, numbers, scalars, sem = refs
    width = slots * BLOCK_PAIRS
    for d, piece in enumerate(pieces):
        numbers[pl.ds(d, 1), :] = piece[0:1, width:].astype(jnp.int32)
    copy = pltpu.make_async_copy(numbers, scalars, sem)
    copy.start()
    copy.wait()
    upper = lax.broadcasted_iota(jnp.int32, (out.shape[0], LANES), 1) // BLOCK_PAIRS
    for d, piece in enumerate(pieces):
        for tile in range(slots // 2):
            value = piece[:, tile * LANES : (tile + 1) * LANES]
            turned = pltpu.roll(value, BLOCK_PAIRS, 1)
            for side in range(2):
                block = scalars[d, 2 * tile + side]
                there = (jnp.maximum(block, 0) // 2) * LANES
                pltpu.store(
                    out.at[:, pl.ds(pl.multiple_of(there, LANES), LANES)],
                    jnp.where(block % 2 == side, value, turned),
                    mask=upper == jnp.where(block >= 0, block % 2, 2),
                )


def placed_rows(pieces, slots, blocks):
    rows = pieces[0].shape[0]
    vmem = pl.BlockSpec(memory_space=pltpu.VMEM)
    return pl.pallas_call(
        functools.partial(place_kernel, slots),
        out_shape=jax.ShapeDtypeStruct((rows, blocks * BLOCK_PAIRS), jnp.float32),
        in_specs=[vmem] * len(pieces),
        out_specs=vmem,
        scratch_shapes=[
            pltpu.VMEM((len(pieces), LANES), jnp.int32),
            pltpu.SMEM((len(pieces), LANES), jnp.int32),
            pltpu.SemaphoreType.DMA,
        ],
        compiler_params=pltpu.CompilerParams(vmem_limit_bytes=8 * MIB),
    )(*pieces)


def merge_kernel(count, mine_from, mine, theirs, ids, *outs):
    width = mine.shape[1]
    rows = outs[0].shape[0]
    for d in range(count):
        here = pl.ds(d * rows, rows)
        outs[d][:, :width] = mine[pl.ds(mine_from + d * rows, rows), :] + theirs[here, :]
        outs[d][:, width:] = jnp.broadcast_to(ids[...], (rows, LANES))


def merged(mine, mine_from, theirs, ids, count):
    vmem = pl.BlockSpec(memory_space=pltpu.VMEM)
    rows = theirs.shape[0] // count
    one = jax.ShapeDtypeStruct((rows, mine.shape[1] + LANES), jnp.float32)
    return pl.pallas_call(
        functools.partial(merge_kernel, count, mine_from),
        out_shape=[one] * count,
        in_specs=[vmem] * 3,
        out_specs=[vmem] * count,
        compiler_params=pltpu.CompilerParams(vmem_limit_bytes=8 * MIB),
    )(mine, theirs, ids)


def swap(value, axis, size, far):
    return lax.ppermute(value, axis, [(i, i ^ far) for i in range(size)])


def local(pairs, ranges, integrals, coefficients, ket_shells, block_ids, pair_owner):
    slots = block_ids.shape[0]
    keep, send = half_rows(integrals, coefficients, ket_shells, pair_owner, pairs, ranges)
    rows = keep + swap(send, "rng", ranges, 1)
    each = NIJ // (pairs * ranges)
    numbers = jnp.pad(block_ids.astype(jnp.float32), (0, LANES - slots)).reshape(1, LANES)
    pieces = [None] * pairs
    step = max(pairs // 2, 1)
    for first in range(0, pairs, step)[::-1]:
        last = first + step
        part = rows.reshape(ranges // 2, pairs, each, -1)[:, first:last]
        for bit in range(1, bits(ranges)):
            half = part.shape[0] // 2
            other = swap(part[half:].reshape(-1, part.shape[-1]), "rng", ranges, 1 << bit)
            if half > 1:
                part = part[:half] + other.reshape(part[half:].shape)
        parts = merged(rows[first * each : last * each], 0, other, numbers, last - first)
        for at in range(last - first):
            d = first + at
            pieces[d] = swap(parts[at], "pair", pairs, d) if d else parts[at]
    return placed_rows(pieces, slots, slots * pairs // 2)


def solution(mesh):
    placed = (
        P(("grp", "pair"), "rng"),
        P("grp", None),
        P(("grp", "rng"), None),
        P(("grp", "pair")),
        P(),
    )
    return jax.shard_map(
        functools.partial(local, mesh.shape["pair"], mesh.shape["rng"]),
        mesh=mesh,
        in_specs=placed,
        out_specs=P(("grp", "pair", "rng"), None),
        check_vma=False,
    )
```

```python
import functools
import jax
import jax.numpy as jnp
from jax import lax
from jax.experimental import pallas as pl
from jax.experimental.pallas import tpu as pltpu
from jax.sharding import PartitionSpec as P

SHELL = 8
BLOCK_PAIRS = 64
NOCC = 16
NIJ = 256
LANES = 128
STEPS = 4
MIB = 1 << 20


def bits(size):
    return size.bit_length() - 1


def order_kernel(pairs, ranges, moved):
    me_pair, me_range = lax.axis_index("pair"), lax.axis_index("rng")
    rows_each = NIJ // (pairs * ranges)
    place = lax.broadcasted_iota(jnp.int32, (SHELL, NIJ), 1)
    inner = place % rows_each
    far_pair = (place // rows_each) % pairs
    order = place // (rows_each * pairs)
    far_range = jnp.zeros_like(order)
    for bit in range(bits(ranges)):
        far_range = far_range + (((order >> (bits(ranges) - 1 - bit)) & 1) << bit)
    target = ((far_pair ^ me_pair) * ranges + (far_range ^ me_range)) * rows_each + inner
    row = lax.broadcasted_iota(jnp.int32, (NIJ, NIJ), 0)
    moved[...] = (row == target[0:1, :]).astype(jnp.bfloat16)


def order_of(pairs, ranges):
    return pl.pallas_call(
        functools.partial(order_kernel, pairs, ranges),
        out_shape=jax.ShapeDtypeStruct((NIJ, NIJ), jnp.bfloat16),
        out_specs=pl.BlockSpec(memory_space=pltpu.VMEM),
        compiler_params=pltpu.CompilerParams(vmem_limit_bytes=8 * MIB),
        cost_estimate=pl.CostEstimate(flops=10**10, bytes_accessed=NIJ * NIJ * 2, transcendentals=0),
    )()


def half_rows_kernel(
    shells_at, owner_at, coef_at, moved, integrals, keep, send, shells, owner, coef,
    table, lam, sig, cols, held, small, sems,
):
    steps = sems.shape[0]
    depth = held.shape[1] // steps
    kets = cols.shape[0] // BLOCK_PAIRS

    def fetch(step):
        here = pl.ds(step * depth, depth)
        return pltpu.make_async_copy(integrals.at[:, here], held.at[:, here], sems.at[step])

    tables = [
        pltpu.make_async_copy(shells_at, shells, small.at[0]),
        pltpu.make_async_copy(owner_at, owner, small.at[1]),
        pltpu.make_async_copy(coef_at, coef, small.at[2]),
    ]
    for copy in tables:
        copy.start()
    for step in range(steps):
        fetch(step).start()

    orbital = lax.broadcasted_iota(jnp.int32, (NOCC, NIJ), 0)
    for copy in tables:
        copy.wait()
    picks = jnp.concatenate(
        [
            (owner[...] // NOCC == orbital).astype(jnp.bfloat16),
            (owner[...] % NOCC == orbital).astype(jnp.bfloat16),
        ],
        axis=0,
    )
    picks = jnp.dot(picks, moved[...], preferred_element_type=jnp.float32).astype(jnp.bfloat16)

    table[...] = coef[...].astype(jnp.float32).T

    for k in range(kets):
        here = pl.ds(k * SHELL, SHELL)
        lam[here, :NOCC] = table[pl.ds(pl.multiple_of(shells[0, k] * SHELL, SHELL), SHELL), :]
        sig[here, :NOCC] = table[pl.ds(pl.multiple_of(shells[1, k] * SHELL, SHELL), SHELL), :]
    lam[...] = jnp.dot(
        lam[:, :NOCC].astype(jnp.bfloat16), picks[:NOCC], preferred_element_type=jnp.float32
    )
    sig[...] = jnp.dot(
        sig[:, :NOCC].astype(jnp.bfloat16), picks[NOCC:], preferred_element_type=jnp.float32
    )
    each = kets // steps
    for step in range(steps):
        for k in range(step * each, (step + 1) * each):
            here = pl.ds(k * SHELL, SHELL)
            both = lam[here, :][:, None, :] * sig[here, :][None, :, :]
            cols[pl.ds(k * BLOCK_PAIRS, BLOCK_PAIRS), :] = both.reshape(BLOCK_PAIRS, NIJ).astype(
                jnp.bfloat16
            )
        fetch(step).wait()
        here = pl.ds(step * depth, depth)
        part = lax.dot_general(
            cols[here, :], held[:, here], (((0,), (1,)), ((), ())),
            preferred_element_type=jnp.float32,
        )
        for at, out in enumerate((keep, send)):
            half = part[at * (NIJ // 2) : (at + 1) * (NIJ // 2)]
            out[...] = half if step == 0 else out[...] + half


def half_rows(integrals, coefficients, ket_shells, pair_owner, pairs, ranges):
    rows, depth = integrals.shape
    kets = ket_shells.shape[0]
    half = jax.ShapeDtypeStruct((NIJ // 2, rows), jnp.float32)
    vmem = pl.BlockSpec(memory_space=pltpu.VMEM)
    return pl.pallas_call(
        half_rows_kernel,
        out_shape=(half, half),
        in_specs=[pl.BlockSpec(memory_space=pl.ANY)] * 3
        + [vmem, pl.BlockSpec(memory_space=pl.ANY)],
        out_specs=(vmem, vmem),
        scratch_shapes=[
            pltpu.SMEM((2, kets), jnp.int32),
            pltpu.VMEM((1, NIJ), jnp.int32),
            pltpu.VMEM((NOCC, coefficients.shape[0]), jnp.bfloat16),
            pltpu.VMEM((coefficients.shape[0], NOCC), jnp.float32),
            pltpu.VMEM((kets * SHELL, NIJ), jnp.float32),
            pltpu.VMEM((kets * SHELL, NIJ), jnp.float32),
            pltpu.VMEM((depth, NIJ), jnp.bfloat16),
            pltpu.VMEM((rows, depth), jnp.bfloat16),
            pltpu.SemaphoreType.DMA((3,)),
            pltpu.SemaphoreType.DMA((STEPS,)),
        ],
        compiler_params=pltpu.CompilerParams(vmem_limit_bytes=52 * MIB),
    )(ket_shells.T, pair_owner.reshape(1, NIJ), coefficients.T, order_of(pairs, ranges), integrals)


def place_kernel(slots, *refs):
    *pieces, out, numbers, scalars, sem = refs
    width = slots * BLOCK_PAIRS
    for d, piece in enumerate(pieces):
        numbers[pl.ds(d, 1), :] = piece[0:1, width:].astype(jnp.int32)
    copy = pltpu.make_async_copy(numbers, scalars, sem)
    copy.start()
    copy.wait()
    upper = lax.broadcasted_iota(jnp.int32, (out.shape[0], LANES), 1) // BLOCK_PAIRS
    for d, piece in enumerate(pieces):
        for tile in range(slots // 2):
            value = piece[:, tile * LANES : (tile + 1) * LANES]
            turned = pltpu.roll(value, BLOCK_PAIRS, 1)
            for side in range(2):
                block = scalars[d, 2 * tile + side]
                there = (jnp.maximum(block, 0) // 2) * LANES
                pltpu.store(
                    out.at[:, pl.ds(pl.multiple_of(there, LANES), LANES)],
                    jnp.where(block % 2 == side, value, turned),
                    mask=upper == jnp.where(block >= 0, block % 2, 2),
                )


def placed_rows(pieces, slots, blocks):
    rows = pieces[0].shape[0]
    vmem = pl.BlockSpec(memory_space=pltpu.VMEM)
    return pl.pallas_call(
        functools.partial(place_kernel, slots),
        out_shape=jax.ShapeDtypeStruct((rows, blocks * BLOCK_PAIRS), jnp.float32),
        in_specs=[vmem] * len(pieces),
        out_specs=vmem,
        scratch_shapes=[
            pltpu.VMEM((len(pieces), LANES), jnp.int32),
            pltpu.SMEM((len(pieces), LANES), jnp.int32),
            pltpu.SemaphoreType.DMA,
        ],
        compiler_params=pltpu.CompilerParams(vmem_limit_bytes=8 * MIB),
    )(*pieces)


def sum_kernel(spans, mine, theirs, earlier, lower, upper):
    half = len(spans) // 2
    for at, (start, size) in enumerate(spans):
        out, place = (lower, at) if at < half else (upper, at - half)
        here = pl.ds(start, size)
        out[pl.ds(place * size, size), :] = mine[here, :] + theirs[here, :]


def summed(mine, theirs, earlier, spans):
    vmem = pl.BlockSpec(memory_space=pltpu.VMEM)
    rows = sum(size for _, size in spans) // 2
    half = jax.ShapeDtypeStruct((rows, mine.shape[1]), jnp.float32)
    return pl.pallas_call(
        functools.partial(sum_kernel, spans),
        out_shape=[half] * 2,
        in_specs=[vmem] * 2 + [pl.BlockSpec(memory_space=pl.ANY)],
        out_specs=[vmem] * 2,
        compiler_params=pltpu.CompilerParams(vmem_limit_bytes=8 * MIB),
    )(mine, theirs, earlier)


def merge_kernel(count, mine_from, mine, theirs, ids, earlier, *outs):
    width = mine.shape[1]
    rows = outs[0].shape[0]
    for d in range(count):
        here = pl.ds(d * rows, rows)
        outs[d][:, :width] = mine[pl.ds(mine_from + d * rows, rows), :] + theirs[here, :]
        outs[d][:, width:] = jnp.broadcast_to(ids[...], (rows, LANES))


def merged(mine, mine_from, theirs, ids, earlier, count):
    vmem = pl.BlockSpec(memory_space=pltpu.VMEM)
    rows = theirs.shape[0] // count
    one = jax.ShapeDtypeStruct((rows, mine.shape[1] + LANES), jnp.float32)
    return pl.pallas_call(
        functools.partial(merge_kernel, count, mine_from),
        out_shape=[one] * count,
        in_specs=[vmem] * 3 + [pl.BlockSpec(memory_space=pl.ANY)],
        out_specs=[vmem] * count,
        compiler_params=pltpu.CompilerParams(vmem_limit_bytes=8 * MIB),
    )(mine, theirs, ids, earlier)


def swap(value, axis, size, far):
    return lax.ppermute(value, axis, [(i, i ^ far) for i in range(size)])


def local(pairs, ranges, integrals, coefficients, ket_shells, block_ids, pair_owner):
    slots = block_ids.shape[0]
    keep, send = half_rows(integrals, coefficients, ket_shells, pair_owner, pairs, ranges)
    across = swap(send, "rng", ranges, 1)
    each = NIJ // (pairs * ranges)
    numbers = jnp.pad(block_ids.astype(jnp.float32), (0, LANES - slots)).reshape(1, LANES)
    step = max(pairs // 2, 1)
    size = step * each
    halves = []
    earlier = across
    for first in range(0, pairs, step)[::-1]:
        spans = tuple(((o * pairs + first) * each, size) for o in range(ranges // 2))
        lower, upper = summed(keep, across, earlier, spans)
        halves.append((first, lower, upper))
        earlier = lower
    pieces = [None] * pairs
    earlier = numbers
    for first, lower, upper in halves:
        for bit in range(1, bits(ranges)):
            other = swap(upper, "rng", ranges, 1 << bit)
            if bit < bits(ranges) - 1:
                lower = lower + other
                lower, upper = jnp.split(lower, 2)
        parts = merged(lower, 0, other, numbers, earlier, step)
        earlier = parts[0]
        for at in range(step):
            d = first + at
            pieces[d] = swap(parts[at], "pair", pairs, d) if d else parts[at]
    pieces = pieces[:1] + pieces[step:] + pieces[1:step]
    return placed_rows(pieces, slots, slots * pairs // 2)


def solution(mesh):
    placed = (
        P(("grp", "pair"), "rng"),
        P("grp", None),
        P(("grp", "rng"), None),
        P(("grp", "pair")),
        P(),
    )
    return jax.shard_map(
        functools.partial(local, mesh.shape["pair"], mesh.shape["rng"]),
        mesh=mesh,
        in_specs=placed,
        out_specs=P(("grp", "pair", "rng"), None),
        check_vma=False,
    )
```

```python
import functools
import jax
import jax.numpy as jnp
from jax import lax
from jax.experimental import pallas as pl
from jax.experimental.pallas import tpu as pltpu
from jax.sharding import PartitionSpec as P

SHELL = 8
BLOCK_PAIRS = 64
NOCC = 16
NIJ = 256
LANES = 128
STEPS = 4
MIB = 1 << 20


def bits(size):
    return size.bit_length() - 1


def order_kernel(pairs, ranges, moved):
    me_pair, me_range = lax.axis_index("pair"), lax.axis_index("rng")
    rows_each = NIJ // (pairs * ranges)
    place = lax.broadcasted_iota(jnp.int32, (SHELL, NIJ), 1)
    inner = place % rows_each
    block = place // rows_each
    low = block % (pairs // 2)
    block = block // (pairs // 2)
    far_range = block // ranges
    for bit in range(1, bits(ranges)):
        far_range = far_range + (((block >> (bits(ranges) - 1 - bit)) & 1) << bit)
    far_pair = low + ((block // (ranges // 2)) % 2) * (pairs // 2)
    target = ((far_pair ^ me_pair) * ranges + (far_range ^ me_range)) * rows_each + inner
    row = lax.broadcasted_iota(jnp.int32, (NIJ, NIJ), 0)
    moved[...] = (row == target[0:1, :]).astype(jnp.bfloat16)


def order_of(pairs, ranges):
    return pl.pallas_call(
        functools.partial(order_kernel, pairs, ranges),
        out_shape=jax.ShapeDtypeStruct((NIJ, NIJ), jnp.bfloat16),
        out_specs=pl.BlockSpec(memory_space=pltpu.VMEM),
        compiler_params=pltpu.CompilerParams(vmem_limit_bytes=8 * MIB),
        cost_estimate=pl.CostEstimate(flops=10**10, bytes_accessed=NIJ * NIJ * 2, transcendentals=0),
    )()


def half_rows_kernel(
    shells_at, owner, coef, moved, integrals, keep_near, keep_far, send_near, send_far, shells,
    table, lam, sig, cols, held, small, sems,
):
    outs = keep_near, keep_far, send_near, send_far
    steps = sems.shape[0]
    depth = held.shape[1] // steps
    kets = cols.shape[0] // BLOCK_PAIRS

    def fetch(step):
        here = pl.ds(step * depth, depth)
        return pltpu.make_async_copy(integrals.at[:, here], held.at[:, here], sems.at[step])

    copy = pltpu.make_async_copy(shells_at, shells, small)
    copy.start()
    for step in range(steps):
        fetch(step).start()

    orbital = lax.broadcasted_iota(jnp.int32, (NOCC, NIJ), 0)
    picks = jnp.concatenate(
        [
            (owner[...] // NOCC == orbital).astype(jnp.bfloat16),
            (owner[...] % NOCC == orbital).astype(jnp.bfloat16),
        ],
        axis=0,
    )
    picks = jnp.dot(picks, moved[...], preferred_element_type=jnp.float32).astype(jnp.bfloat16)

    table[...] = coef[...].astype(jnp.float32).T
    copy.wait()

    for k in range(kets):
        here = pl.ds(k * SHELL, SHELL)
        lam[here, :NOCC] = table[pl.ds(pl.multiple_of(shells[0, k] * SHELL, SHELL), SHELL), :]
        sig[here, :NOCC] = table[pl.ds(pl.multiple_of(shells[1, k] * SHELL, SHELL), SHELL), :]
    lam[...] = jnp.dot(
        lam[:, :NOCC].astype(jnp.bfloat16), picks[:NOCC], preferred_element_type=jnp.float32
    )
    sig[...] = jnp.dot(
        sig[:, :NOCC].astype(jnp.bfloat16), picks[NOCC:], preferred_element_type=jnp.float32
    )
    each = kets // steps
    for step in range(steps):
        for k in range(step * each, (step + 1) * each):
            here = pl.ds(k * SHELL, SHELL)
            both = lam[here, :][:, None, :] * sig[here, :][None, :, :]
            cols[pl.ds(k * BLOCK_PAIRS, BLOCK_PAIRS), :] = both.reshape(BLOCK_PAIRS, NIJ).astype(
                jnp.bfloat16
            )
        fetch(step).wait()
        here = pl.ds(step * depth, depth)
        part = lax.dot_general(
            cols[here, :], held[:, here], (((0,), (1,)), ((), ())),
            preferred_element_type=jnp.float32,
        )
        for at, out in enumerate(outs):
            rows = part[at * (NIJ // 4) : (at + 1) * (NIJ // 4)]
            out[...] = rows if step == 0 else out[...] + rows


def half_rows(integrals, coefficients, ket_shells, pair_owner, pairs, ranges):
    rows, depth = integrals.shape
    kets = ket_shells.shape[0]
    part = jax.ShapeDtypeStruct((NIJ // 4, rows), jnp.float32)
    vmem = pl.BlockSpec(memory_space=pltpu.VMEM)
    hbm = pl.BlockSpec(memory_space=pl.ANY)
    return pl.pallas_call(
        half_rows_kernel,
        out_shape=[part] * 4,
        in_specs=[hbm, vmem, vmem, vmem, hbm],
        out_specs=[vmem] * 4,
        scratch_shapes=[
            pltpu.SMEM((2, kets), jnp.int32),
            pltpu.VMEM((coefficients.shape[0], NOCC), jnp.float32),
            pltpu.VMEM((kets * SHELL, NIJ), jnp.float32),
            pltpu.VMEM((kets * SHELL, NIJ), jnp.float32),
            pltpu.VMEM((depth, NIJ), jnp.bfloat16),
            pltpu.VMEM((rows, depth), jnp.bfloat16),
            pltpu.SemaphoreType.DMA,
            pltpu.SemaphoreType.DMA((STEPS,)),
        ],
        compiler_params=pltpu.CompilerParams(vmem_limit_bytes=52 * MIB),
    )(ket_shells.T, pair_owner.reshape(1, NIJ), coefficients.T, order_of(pairs, ranges), integrals)


def place_kernel(slots, *refs):
    *pieces, out, numbers, scalars, sem = refs
    width = slots * BLOCK_PAIRS
    for d, piece in enumerate(pieces):
        numbers[pl.ds(d, 1), :] = piece[0:1, width:].astype(jnp.int32)
    copy = pltpu.make_async_copy(numbers, scalars, sem)
    copy.start()
    copy.wait()
    upper = lax.broadcasted_iota(jnp.int32, (out.shape[0], LANES), 1) // BLOCK_PAIRS
    for d, piece in enumerate(pieces):
        for tile in range(slots // 2):
            value = piece[:, tile * LANES : (tile + 1) * LANES]
            turned = pltpu.roll(value, BLOCK_PAIRS, 1)
            for side in range(2):
                block = scalars[d, 2 * tile + side]
                there = (jnp.maximum(block, 0) // 2) * LANES
                pltpu.store(
                    out.at[:, pl.ds(pl.multiple_of(there, LANES), LANES)],
                    jnp.where(block % 2 == side, value, turned),
                    mask=upper == jnp.where(block >= 0, block % 2, 2),
                )


def placed_rows(pieces, slots, blocks):
    rows = pieces[0].shape[0]
    vmem = pl.BlockSpec(memory_space=pltpu.VMEM)
    return pl.pallas_call(
        functools.partial(place_kernel, slots),
        out_shape=jax.ShapeDtypeStruct((rows, blocks * BLOCK_PAIRS), jnp.float32),
        in_specs=[vmem] * len(pieces),
        out_specs=vmem,
        scratch_shapes=[
            pltpu.VMEM((len(pieces), LANES), jnp.int32),
            pltpu.SMEM((len(pieces), LANES), jnp.int32),
            pltpu.SemaphoreType.DMA,
        ],
        compiler_params=pltpu.CompilerParams(vmem_limit_bytes=8 * MIB),
    )(*pieces)


def sum_kernel(spans, mine, theirs, earlier, lower, upper):
    half = len(spans) // 2
    for at, (start, size) in enumerate(spans):
        out, place = (lower, at) if at < half else (upper, at - half)
        here = pl.ds(start, size)
        out[pl.ds(place * size, size), :] = mine[here, :] + theirs[here, :]


def summed(mine, theirs, earlier, spans, cost):
    vmem = pl.BlockSpec(memory_space=pltpu.VMEM)
    rows = sum(size for _, size in spans) // 2
    half = jax.ShapeDtypeStruct((rows, mine.shape[1]), jnp.float32)
    return pl.pallas_call(
        functools.partial(sum_kernel, spans),
        out_shape=[half] * 2,
        in_specs=[vmem] * 2 + [pl.BlockSpec(memory_space=pl.ANY)],
        out_specs=[vmem] * 2,
        cost_estimate=pl.CostEstimate(flops=cost, bytes_accessed=0, transcendentals=0),
        compiler_params=pltpu.CompilerParams(vmem_limit_bytes=8 * MIB),
    )(mine, theirs, earlier)


def merge_kernel(count, mine, theirs, ids, earlier, *outs):
    width = mine.shape[1]
    rows = outs[0].shape[0]
    for d in range(count):
        here = pl.ds(d * rows, rows)
        outs[d][:, :width] = mine[here, :] + theirs[here, :]
        outs[d][:, width:] = jnp.broadcast_to(ids[...], (rows, LANES))


def merged(mine, theirs, ids, earlier, count, cost):
    vmem = pl.BlockSpec(memory_space=pltpu.VMEM)
    rows = theirs.shape[0] // count
    one = jax.ShapeDtypeStruct((rows, mine.shape[1] + LANES), jnp.float32)
    return pl.pallas_call(
        functools.partial(merge_kernel, count),
        out_shape=[one] * count,
        in_specs=[vmem] * 3 + [pl.BlockSpec(memory_space=pl.ANY)],
        out_specs=[vmem] * count,
        cost_estimate=pl.CostEstimate(flops=cost, bytes_accessed=0, transcendentals=0),
        compiler_params=pltpu.CompilerParams(vmem_limit_bytes=8 * MIB),
    )(mine, theirs, ids, earlier)


def swap(value, axis, size, far):
    return lax.ppermute(value, axis, [(i, i ^ far) for i in range(size)])


def local(pairs, ranges, integrals, coefficients, ket_shells, block_ids, pair_owner):
    slots = block_ids.shape[0]
    near, far, send_near, send_far = half_rows(
        integrals, coefficients, ket_shells, pair_owner, pairs, ranges
    )
    far = far, swap(send_far, "rng", ranges, 1)
    near = near, swap(send_near, "rng", ranges, 1)
    each = NIJ // (pairs * ranges)
    numbers = jnp.pad(block_ids.astype(jnp.float32), (0, LANES - slots)).reshape(1, LANES)
    step = pairs // 2
    some = max(step // 2, 1)
    groups = [(far, at, step, some) for at in range(0, step, some)] + [(near, 0, 0, step)]
    halves = []
    earlier = far[1]
    for sums, at, base, count in groups:
        spans = tuple(
            ((o * step + at) * each, count * each) for o in range(ranges // 2)
        )
        lower, upper = summed(*sums, earlier, spans, 10**6 if base else 5 * 10**8)
        halves.append((base + at, count, lower, upper))
        earlier = lower
    pieces = [None] * pairs
    earlier = numbers
    for first, count, lower, upper in halves:
        for bit in range(1, bits(ranges)):
            other = swap(upper, "rng", ranges, 1 << bit)
            if bit < bits(ranges) - 1:
                lower = lower + other
                lower, upper = jnp.split(lower, 2)
        parts = merged(lower, other, numbers, earlier, count, 10**9 if first == step else 10**10)
        earlier = parts[0]
        for at in range(count):
            d = first + at
            pieces[d] = swap(parts[at], "pair", pairs, d) if d else parts[at]
    pieces = pieces[:1] + pieces[step:] + pieces[1:step]
    return placed_rows(pieces, slots, slots * pairs // 2)


def solution(mesh):
    placed = (
        P(("grp", "pair"), "rng"),
        P("grp", None),
        P(("grp", "rng"), None),
        P(("grp", "pair")),
        P(),
    )
    return jax.shard_map(
        functools.partial(local, mesh.shape["pair"], mesh.shape["rng"]),
        mesh=mesh,
        in_specs=placed,
        out_specs=P(("grp", "pair", "rng"), None),
        check_vma=False,
    )
```

```python
import functools
import jax
import jax.numpy as jnp
from jax import lax
from jax.experimental import pallas as pl
from jax.experimental.pallas import tpu as pltpu
from jax.sharding import PartitionSpec as P

SHELL = 8
BLOCK_PAIRS = 64
NOCC = 16
NIJ = 256
LANES = 128
CHUNKS = 4, 4, 4, 4
MIB = 1 << 20


def bits(size):
    return size.bit_length() - 1


def order_kernel(pairs, ranges, moved):
    me_pair, me_range = lax.axis_index("pair"), lax.axis_index("rng")
    rows_each = NIJ // (pairs * ranges)
    place = lax.broadcasted_iota(jnp.int32, (SHELL, NIJ), 1)
    inner = place % rows_each
    block = place // rows_each
    step, some, chips = pairs // 2, max(pairs // 4, 1), ranges // 2
    core = block // (pairs * chips)
    high = (block // (step * chips)) % 2
    block = block % (step * chips)
    far = high == 1
    low = jnp.where(far, (block // (some * chips)) * some + block % some, block % step)
    order = jnp.where(far, (block // some) % chips, block // step)
    far_range = core
    for bit in range(1, bits(ranges)):
        far_range = far_range + (((order >> (bits(ranges) - 1 - bit)) & 1) << bit)
    far_pair = low + high * step
    target = ((far_pair ^ me_pair) * ranges + (far_range ^ me_range)) * rows_each + inner
    row = lax.broadcasted_iota(jnp.int32, (NIJ, NIJ), 0)
    moved[...] = (row == target[0:1, :]).astype(jnp.bfloat16)


def order_of(pairs, ranges):
    return pl.pallas_call(
        functools.partial(order_kernel, pairs, ranges),
        out_shape=jax.ShapeDtypeStruct((NIJ, NIJ), jnp.bfloat16),
        out_specs=pl.BlockSpec(memory_space=pltpu.VMEM),
        compiler_params=pltpu.CompilerParams(vmem_limit_bytes=8 * MIB),
        cost_estimate=pl.CostEstimate(flops=10**10, bytes_accessed=NIJ * NIJ * 2, transcendentals=0),
    )()


def half_rows_kernel(spans, shells_at, owner, coef, moved, integrals, *refs):
    outs, (shells, table, lam, sig, cols, held, small, sems) = refs[:-8], refs[-8:]
    steps = len(spans)

    def fetch(step):
        here = pl.ds(*spans[step])
        return pltpu.make_async_copy(integrals.at[:, here], held.at[:, here], sems.at[step])

    copy = pltpu.make_async_copy(shells_at, shells, small)
    copy.start()
    for step in range(steps):
        fetch(step).start()

    orbital = lax.broadcasted_iota(jnp.int32, (NOCC, NIJ), 0)
    picks = jnp.concatenate(
        [
            (owner[...] // NOCC == orbital).astype(jnp.bfloat16),
            (owner[...] % NOCC == orbital).astype(jnp.bfloat16),
        ],
        axis=0,
    )
    picks = jnp.dot(picks, moved[...], preferred_element_type=jnp.float32).astype(jnp.bfloat16)

    table[...] = coef[...].astype(jnp.float32).T
    copy.wait()

    for k in range(lam.shape[0] // SHELL):
        here = pl.ds(k * SHELL, SHELL)
        lam[here, :NOCC] = table[pl.ds(pl.multiple_of(shells[0, k] * SHELL, SHELL), SHELL), :]
        sig[here, :NOCC] = table[pl.ds(pl.multiple_of(shells[1, k] * SHELL, SHELL), SHELL), :]
    lam[...] = jnp.dot(
        lam[:, :NOCC].astype(jnp.bfloat16), picks[:NOCC], preferred_element_type=jnp.float32
    )
    sig[...] = jnp.dot(
        sig[:, :NOCC].astype(jnp.bfloat16), picks[NOCC:], preferred_element_type=jnp.float32
    )
    for step in range(steps):
        start, size = spans[step]
        for k in range(start // BLOCK_PAIRS, (start + size) // BLOCK_PAIRS):
            here = pl.ds(k * SHELL, SHELL)
            both = lam[here, :][:, None, :] * sig[here, :][None, :, :]
            cols[pl.ds(k * BLOCK_PAIRS, BLOCK_PAIRS), :] = both.reshape(BLOCK_PAIRS, NIJ).astype(
                jnp.bfloat16
            )
        fetch(step).wait()
        part = lax.dot_general(
            cols[pl.ds(start, size), :], held[:, pl.ds(start, size)], (((0,), (1,)), ((), ())),
            preferred_element_type=jnp.float32,
        )
        at = 0
        for out in outs:
            rows = part[at : at + out.shape[0]]
            out[...] = rows if step == 0 else out[...] + rows
            at += out.shape[0]


def half_rows(integrals, coefficients, ket_shells, pair_owner, pairs, ranges, sizes):
    rows, depth = integrals.shape
    kets = ket_shells.shape[0]
    parts = [jax.ShapeDtypeStruct((size, rows), jnp.float32) for size in sizes * 2]
    ends = [sum(CHUNKS[:at]) * depth // 16 for at in range(len(CHUNKS) + 1)]
    spans = [(start, end - start) for start, end in zip(ends, ends[1:])]
    vmem = pl.BlockSpec(memory_space=pltpu.VMEM)
    hbm = pl.BlockSpec(memory_space=pl.ANY)
    return pl.pallas_call(
        functools.partial(half_rows_kernel, spans),
        out_shape=parts,
        in_specs=[hbm, vmem, vmem, vmem, hbm],
        out_specs=[vmem] * len(parts),
        scratch_shapes=[
            pltpu.SMEM((2, kets), jnp.int32),
            pltpu.VMEM((coefficients.shape[0], NOCC), jnp.float32),
            pltpu.VMEM((kets * SHELL, NIJ), jnp.float32),
            pltpu.VMEM((kets * SHELL, NIJ), jnp.float32),
            pltpu.VMEM((depth, NIJ), jnp.bfloat16),
            pltpu.VMEM((rows, depth), jnp.bfloat16),
            pltpu.SemaphoreType.DMA,
            pltpu.SemaphoreType.DMA((len(spans),)),
        ],
        compiler_params=pltpu.CompilerParams(vmem_limit_bytes=52 * MIB),
    )(ket_shells.T, pair_owner.reshape(1, NIJ), coefficients.T, order_of(pairs, ranges), integrals)


def place_kernel(slots, count, *refs):
    pieces, before = refs[:count], refs[count:-4]
    out, numbers, scalars, sem = refs[-4:]
    rows = out.shape[0]
    for d, piece in enumerate(pieces):
        numbers[pl.ds(d, 1), :] = piece[pl.ds(slots // 2 * rows, 1), :].astype(jnp.int32)
    copy = pltpu.make_async_copy(numbers, scalars, sem)
    copy.start()
    for done in before:
        out[...] = done[...]
    copy.wait()
    upper = lax.broadcasted_iota(jnp.int32, (out.shape[0], LANES), 1) // BLOCK_PAIRS
    for d, piece in enumerate(pieces):
        for tile in range(slots // 2):
            value = piece[pl.ds(tile * rows, rows), :]
            turned = pltpu.roll(value, BLOCK_PAIRS, 1)
            for side in range(2):
                block = scalars[d, 2 * tile + side]
                there = (jnp.maximum(block, 0) >> 1) * LANES
                pltpu.store(
                    out.at[:, pl.ds(pl.multiple_of(there, LANES), LANES)],
                    jnp.where((block & 1) == side, value, turned),
                    mask=upper == jnp.where(block >= 0, block & 1, 2),
                )


def placed_rows(pieces, before, slots, blocks):
    rows = pieces[0].shape[0] // (slots // 2)
    vmem = pl.BlockSpec(memory_space=pltpu.VMEM)
    return pl.pallas_call(
        functools.partial(place_kernel, slots, len(pieces)),
        out_shape=jax.ShapeDtypeStruct((rows, blocks * BLOCK_PAIRS), jnp.float32),
        in_specs=[vmem] * (len(pieces) + len(before)),
        out_specs=vmem,
        scratch_shapes=[
            pltpu.VMEM((len(pieces), LANES), jnp.int32),
            pltpu.SMEM((len(pieces), LANES), jnp.int32),
            pltpu.SemaphoreType.DMA,
        ],
        compiler_params=pltpu.CompilerParams(vmem_limit_bytes=8 * MIB),
    )(*pieces, *before)


def sum_kernel(mine, theirs, earlier, lower, upper):
    half = lower.shape[0]
    lower[...] = mine[:half] + theirs[:half]
    upper[...] = mine[half:] + theirs[half:]


def summed(mine, theirs, earlier, cost):
    vmem = pl.BlockSpec(memory_space=pltpu.VMEM)
    half = jax.ShapeDtypeStruct((mine.shape[0] // 2, mine.shape[1]), jnp.float32)
    return pl.pallas_call(
        sum_kernel,
        out_shape=[half] * 2,
        in_specs=[vmem] * 2 + [pl.BlockSpec(memory_space=pl.ANY)],
        out_specs=[vmem] * 2,
        cost_estimate=pl.CostEstimate(flops=cost, bytes_accessed=0, transcendentals=0),
        compiler_params=pltpu.CompilerParams(vmem_limit_bytes=8 * MIB),
    )(mine, theirs, earlier)


def merge_kernel(count, mine, theirs, ids, earlier, *outs):
    tiles = mine.shape[1] // LANES
    rows = mine.shape[0] // count
    for d in range(count):
        here = pl.ds(d * rows, rows)
        for tile in range(tiles):
            lanes = pl.ds(tile * LANES, LANES)
            outs[d][pl.ds(tile * rows, rows), :] = mine[here, lanes] + theirs[here, lanes]
        outs[d][pl.ds(tiles * rows, 1), :] = ids[...]


def merged(mine, theirs, ids, earlier, count, cost):
    vmem = pl.BlockSpec(memory_space=pltpu.VMEM)
    rows = theirs.shape[0] // count
    one = jax.ShapeDtypeStruct((rows * (mine.shape[1] // LANES) + 1, LANES), jnp.float32)
    return pl.pallas_call(
        functools.partial(merge_kernel, count),
        out_shape=[one] * count,
        in_specs=[vmem] * 3 + [pl.BlockSpec(memory_space=pl.ANY)],
        out_specs=[vmem] * count,
        cost_estimate=pl.CostEstimate(flops=cost, bytes_accessed=0, transcendentals=0),
        compiler_params=pltpu.CompilerParams(vmem_limit_bytes=8 * MIB),
    )(mine, theirs, ids, earlier)


def swap(value, axis, size, far):
    return lax.ppermute(value, axis, [(i, i ^ far) for i in range(size)])


def local(pairs, ranges, integrals, coefficients, ket_shells, block_ids, pair_owner):
    slots = block_ids.shape[0]
    each = NIJ // (pairs * ranges)
    step = pairs // 2
    some = max(step // 2, 1)
    groups = [(0, step)] + [(step + at, some) for at in range(0, step, some)]
    sizes = [count * each * (ranges // 2) for _, count in groups]
    parts = half_rows(integrals, coefficients, ket_shells, pair_owner, pairs, ranges, sizes)
    numbers = jnp.pad(block_ids.astype(jnp.float32), (0, LANES - slots)).reshape(1, LANES)
    groups = [
        (first, count, parts[at], parts[at + len(groups)])
        for at, (first, count) in enumerate(groups)
    ]
    groups = [
        (first, count, mine, swap(send, "rng", ranges, 1))
        for first, count, mine, send in groups[1:] + groups[:1]
    ]
    halves = []
    earlier = groups[0][3]
    for first, count, mine, theirs in groups:
        lower, upper = summed(mine, theirs, earlier, 5 * 10**8)
        halves.append((first, count, lower, upper))
        earlier = lower
    pieces = [None] * pairs
    earlier = numbers
    for first, count, lower, upper in halves:
        for bit in range(1, bits(ranges)):
            other = swap(upper, "rng", ranges, 1 << bit)
            if bit < bits(ranges) - 1:
                lower = lower + other
                lower, upper = jnp.split(lower, 2)
        parts = merged(lower, other, numbers, earlier, count, 10**9 if first == step else 2 * 10**9)
        earlier = parts[0]
        for at in range(count):
            d = first + at
            pieces[d] = swap(parts[at], "pair", pairs, d) if d else parts[at]
    blocks = slots * pairs // 2
    early = placed_rows(pieces[:1] + pieces[step:], [], slots, blocks)
    return placed_rows(pieces[1:step], [early], slots, blocks) if step > 1 else early


def solution(mesh):
    placed = (
        P(("grp", "pair"), "rng"),
        P("grp", None),
        P(("grp", "rng"), None),
        P(("grp", "pair")),
        P(),
    )
    return jax.shard_map(
        functools.partial(local, mesh.shape["pair"], mesh.shape["rng"]),
        mesh=mesh,
        in_specs=placed,
        out_specs=P(("grp", "pair", "rng"), None),
        check_vma=False,
    )
```

```python
import functools
import jax
import jax.numpy as jnp
from jax import lax
from jax.experimental import pallas as pl
from jax.experimental.pallas import tpu as pltpu
from jax.sharding import PartitionSpec as P

SHELL = 8
BLOCK_PAIRS = 64
NOCC = 16
NIJ = 256
LANES = 128
CHUNKS = 4, 4, 4, 4
MIB = 1 << 20


def bits(size):
    return size.bit_length() - 1


def order_kernel(pairs, ranges, moved):
    me_pair, me_range = lax.axis_index("pair"), lax.axis_index("rng")
    rows_each = NIJ // (pairs * ranges)
    place = lax.broadcasted_iota(jnp.int32, (SHELL, NIJ), 1)
    inner = place % rows_each
    block = place // rows_each
    step, some, chips = pairs // 2, max(pairs // 4, 1), ranges // 2
    core = block // (pairs * chips)
    high = (block // (step * chips)) % 2
    block = block % (step * chips)
    far = high == 1
    low = jnp.where(far, (block // (some * chips)) * some + block % some, block % step)
    order = jnp.where(far, (block // some) % chips, block // step)
    far_range = core
    for bit in range(1, bits(ranges)):
        far_range = far_range + (((order >> (bits(ranges) - 1 - bit)) & 1) << bit)
    far_pair = low + high * step
    target = ((far_pair ^ me_pair) * ranges + (far_range ^ me_range)) * rows_each + inner
    row = lax.broadcasted_iota(jnp.int32, (NIJ, NIJ), 0)
    moved[...] = (row == target[0:1, :]).astype(jnp.bfloat16)


def order_of(pairs, ranges):
    return pl.pallas_call(
        functools.partial(order_kernel, pairs, ranges),
        out_shape=jax.ShapeDtypeStruct((NIJ, NIJ), jnp.bfloat16),
        out_specs=pl.BlockSpec(memory_space=pltpu.VMEM),
        compiler_params=pltpu.CompilerParams(vmem_limit_bytes=8 * MIB),
        cost_estimate=pl.CostEstimate(flops=10**10, bytes_accessed=NIJ * NIJ * 2, transcendentals=0),
    )()


def half_rows_kernel(spans, shells_at, owner, coef, moved, integrals, *refs):
    outs, (shells, table, lam, sig, cols, held, small, sems) = refs[:-8], refs[-8:]
    steps = len(spans)

    def fetch(step):
        here = pl.ds(*spans[step])
        return pltpu.make_async_copy(integrals.at[:, here], held.at[:, here], sems.at[step])

    copy = pltpu.make_async_copy(shells_at, shells, small)
    copy.start()
    for step in range(steps):
        fetch(step).start()

    orbital = lax.broadcasted_iota(jnp.int32, (NOCC, NIJ), 0)
    picks = jnp.concatenate(
        [
            (owner[...] // NOCC == orbital).astype(jnp.bfloat16),
            (owner[...] % NOCC == orbital).astype(jnp.bfloat16),
        ],
        axis=0,
    )
    picks = jnp.dot(picks, moved[...], preferred_element_type=jnp.float32).astype(jnp.bfloat16)

    table[...] = coef[...].astype(jnp.float32).T
    copy.wait()

    for k in range(lam.shape[0] // SHELL):
        here = pl.ds(k * SHELL, SHELL)
        lam[here, :NOCC] = table[pl.ds(pl.multiple_of(shells[0, k] * SHELL, SHELL), SHELL), :]
        sig[here, :NOCC] = table[pl.ds(pl.multiple_of(shells[1, k] * SHELL, SHELL), SHELL), :]
    lam[...] = jnp.dot(
        lam[:, :NOCC].astype(jnp.bfloat16), picks[:NOCC], preferred_element_type=jnp.float32
    )
    sig[...] = jnp.dot(
        sig[:, :NOCC].astype(jnp.bfloat16), picks[NOCC:], preferred_element_type=jnp.float32
    )
    for step in range(steps):
        start, size = spans[step]
        for k in range(start // BLOCK_PAIRS, (start + size) // BLOCK_PAIRS):
            here = pl.ds(k * SHELL, SHELL)
            both = lam[here, :][:, None, :] * sig[here, :][None, :, :]
            cols[pl.ds(k * BLOCK_PAIRS, BLOCK_PAIRS), :] = both.reshape(BLOCK_PAIRS, NIJ).astype(
                jnp.bfloat16
            )
        fetch(step).wait()
        part = lax.dot_general(
            cols[pl.ds(start, size), :], held[:, pl.ds(start, size)], (((0,), (1,)), ((), ())),
            preferred_element_type=jnp.float32,
        )
        at = 0
        for out in outs:
            rows = part[at : at + out.shape[0]]
            out[...] = rows if step == 0 else out[...] + rows
            at += out.shape[0]


def half_rows(integrals, coefficients, ket_shells, pair_owner, pairs, ranges, sizes):
    rows, depth = integrals.shape
    kets = ket_shells.shape[0]
    parts = [jax.ShapeDtypeStruct((size, rows), jnp.float32) for size in sizes * 2]
    ends = [sum(CHUNKS[:at]) * depth // 16 for at in range(len(CHUNKS) + 1)]
    spans = [(start, end - start) for start, end in zip(ends, ends[1:])]
    vmem = pl.BlockSpec(memory_space=pltpu.VMEM)
    hbm = pl.BlockSpec(memory_space=pl.ANY)
    return pl.pallas_call(
        functools.partial(half_rows_kernel, spans),
        out_shape=parts,
        in_specs=[hbm, vmem, vmem, vmem, hbm],
        out_specs=[vmem] * len(parts),
        scratch_shapes=[
            pltpu.SMEM((2, kets), jnp.int32),
            pltpu.VMEM((coefficients.shape[0], NOCC), jnp.float32),
            pltpu.VMEM((kets * SHELL, NIJ), jnp.float32),
            pltpu.VMEM((kets * SHELL, NIJ), jnp.float32),
            pltpu.VMEM((depth, NIJ), jnp.bfloat16),
            pltpu.VMEM((rows, depth), jnp.bfloat16),
            pltpu.SemaphoreType.DMA,
            pltpu.SemaphoreType.DMA((len(spans),)),
        ],
        compiler_params=pltpu.CompilerParams(vmem_limit_bytes=52 * MIB),
    )(ket_shells.T, pair_owner.reshape(1, NIJ), coefficients.T, order_of(pairs, ranges), integrals)


def place_kernel(slots, count, *refs):
    pieces, before = refs[:count], refs[count:-1]
    out = refs[-1]
    rows = out.shape[0]
    for done in before:
        out[...] = done[...]
    upper = lax.broadcasted_iota(jnp.int32, (out.shape[0], LANES), 1) // BLOCK_PAIRS
    for piece in pieces:
        ids = piece[pl.ds(slots // 2 * rows, 1), :].astype(jnp.int32)
        for tile in range(slots // 2):
            value = piece[pl.ds(tile * rows, rows), :]
            turned = pltpu.roll(value, BLOCK_PAIRS, 1)
            for side in range(2):
                block = ids[0, 2 * tile + side]
                there = (jnp.maximum(block, 0) >> 1) * LANES
                pltpu.store(
                    out.at[:, pl.ds(pl.multiple_of(there, LANES), LANES)],
                    jnp.where((block & 1) == side, value, turned),
                    mask=upper == jnp.where(block >= 0, block & 1, 2),
                )


def placed_rows(pieces, before, slots, blocks):
    rows = pieces[0].shape[0] // (slots // 2)
    vmem = pl.BlockSpec(memory_space=pltpu.VMEM)
    return pl.pallas_call(
        functools.partial(place_kernel, slots, len(pieces)),
        out_shape=jax.ShapeDtypeStruct((rows, blocks * BLOCK_PAIRS), jnp.float32),
        in_specs=[vmem] * (len(pieces) + len(before)),
        out_specs=vmem,
        compiler_params=pltpu.CompilerParams(vmem_limit_bytes=8 * MIB),
    )(*pieces, *before)


def sum_kernel(mine, theirs, earlier, lower, upper):
    half = lower.shape[0]
    lower[...] = mine[:half] + theirs[:half]
    upper[...] = mine[half:] + theirs[half:]


def summed(mine, theirs, earlier, cost):
    vmem = pl.BlockSpec(memory_space=pltpu.VMEM)
    half = jax.ShapeDtypeStruct((mine.shape[0] // 2, mine.shape[1]), jnp.float32)
    return pl.pallas_call(
        sum_kernel,
        out_shape=[half] * 2,
        in_specs=[vmem] * 2 + [pl.BlockSpec(memory_space=pl.ANY)],
        out_specs=[vmem] * 2,
        cost_estimate=pl.CostEstimate(flops=cost, bytes_accessed=0, transcendentals=0),
        compiler_params=pltpu.CompilerParams(vmem_limit_bytes=8 * MIB),
    )(mine, theirs, earlier)


def merge_kernel(count, mine, theirs, ids, earlier, *outs):
    tiles = mine.shape[1] // LANES
    rows = mine.shape[0] // count
    for d in range(count):
        here = pl.ds(d * rows, rows)
        for tile in range(tiles):
            lanes = pl.ds(tile * LANES, LANES)
            outs[d][pl.ds(tile * rows, rows), :] = mine[here, lanes] + theirs[here, lanes]
        outs[d][pl.ds(tiles * rows, 1), :] = ids[...]


def merged(mine, theirs, ids, earlier, count, cost):
    vmem = pl.BlockSpec(memory_space=pltpu.VMEM)
    rows = theirs.shape[0] // count
    one = jax.ShapeDtypeStruct((rows * (mine.shape[1] // LANES) + 1, LANES), jnp.float32)
    return pl.pallas_call(
        functools.partial(merge_kernel, count),
        out_shape=[one] * count,
        in_specs=[vmem] * 3 + [pl.BlockSpec(memory_space=pl.ANY)],
        out_specs=[vmem] * count,
        cost_estimate=pl.CostEstimate(flops=cost, bytes_accessed=0, transcendentals=0),
        compiler_params=pltpu.CompilerParams(vmem_limit_bytes=8 * MIB),
    )(mine, theirs, ids, earlier)


def swap(value, axis, size, far):
    return lax.ppermute(value, axis, [(i, i ^ far) for i in range(size)])


def local(pairs, ranges, integrals, coefficients, ket_shells, block_ids, pair_owner):
    slots = block_ids.shape[0]
    each = NIJ // (pairs * ranges)
    step = pairs // 2
    some = max(step // 2, 1)
    groups = [(0, step)] + [(step + at, some) for at in range(0, step, some)]
    sizes = [count * each * (ranges // 2) for _, count in groups]
    parts = half_rows(integrals, coefficients, ket_shells, pair_owner, pairs, ranges, sizes)
    numbers = jnp.pad(block_ids.astype(jnp.float32), (0, LANES - slots)).reshape(1, LANES)
    groups = [
        (first, count, parts[at], parts[at + len(groups)])
        for at, (first, count) in enumerate(groups)
    ]
    groups = [
        (first, count, mine, swap(send, "rng", ranges, 1))
        for first, count, mine, send in groups[1:] + groups[:1]
    ]
    halves = []
    earlier = groups[0][3]
    for first, count, mine, theirs in groups:
        lower, upper = summed(mine, theirs, earlier, 5 * 10**8)
        halves.append((first, count, lower, upper))
        earlier = lower
    pieces = [None] * pairs
    earlier = numbers
    for first, count, lower, upper in halves:
        for bit in range(1, bits(ranges)):
            other = swap(upper, "rng", ranges, 1 << bit)
            if bit < bits(ranges) - 1:
                lower = lower + other
                lower, upper = jnp.split(lower, 2)
        parts = merged(lower, other, numbers, earlier, count, 10**9 if first == step else 2 * 10**9)
        earlier = parts[0]
        for at in range(count):
            d = first + at
            pieces[d] = swap(parts[at], "pair", pairs, d) if d else parts[at]
    blocks = slots * pairs // 2
    early = placed_rows(pieces[:1] + pieces[step:], [], slots, blocks)
    return placed_rows(pieces[1:step], [early], slots, blocks) if step > 1 else early


def solution(mesh):
    placed = (
        P(("grp", "pair"), "rng"),
        P("grp", None),
        P(("grp", "rng"), None),
        P(("grp", "pair")),
        P(),
    )
    return jax.shard_map(
        functools.partial(local, mesh.shape["pair"], mesh.shape["rng"]),
        mesh=mesh,
        in_specs=placed,
        out_specs=P(("grp", "pair", "rng"), None),
        check_vma=False,
    )
```

```python
import functools
import jax
import jax.numpy as jnp
from jax import lax
from jax.experimental import pallas as pl
from jax.experimental.pallas import tpu as pltpu
from jax.sharding import PartitionSpec as P

SHELL = 8
BLOCK_PAIRS = 64
NOCC = 16
NIJ = 256
LANES = 128
CHUNKS = 4, 4, 4, 4
MIB = 1 << 20


def bits(size):
    return size.bit_length() - 1


def order_kernel(pairs, ranges, moved):
    me_pair, me_range = lax.axis_index("pair"), lax.axis_index("rng")
    rows_each = NIJ // (pairs * ranges)
    place = lax.broadcasted_iota(jnp.int32, (SHELL, NIJ), 1)
    inner = place % rows_each
    block = place // rows_each
    some, chips = max(pairs // 4, 1), ranges // 2
    core = block // (pairs * chips)
    block = block % (pairs * chips)
    order = (block // some) % chips
    far_range = core
    for bit in range(1, bits(ranges)):
        far_range = far_range + (((order >> (bits(ranges) - 1 - bit)) & 1) << bit)
    far_pair = (block // (some * chips)) * some + block % some
    target = ((far_pair ^ me_pair) * ranges + (far_range ^ me_range)) * rows_each + inner
    row = lax.broadcasted_iota(jnp.int32, (NIJ, NIJ), 0)
    moved[...] = (row == target[0:1, :]).astype(jnp.bfloat16)


def order_of(pairs, ranges):
    return pl.pallas_call(
        functools.partial(order_kernel, pairs, ranges),
        out_shape=jax.ShapeDtypeStruct((NIJ, NIJ), jnp.bfloat16),
        out_specs=pl.BlockSpec(memory_space=pltpu.VMEM),
        compiler_params=pltpu.CompilerParams(vmem_limit_bytes=8 * MIB),
        cost_estimate=pl.CostEstimate(flops=10**10, bytes_accessed=NIJ * NIJ * 2, transcendentals=0),
    )()


def half_rows_kernel(spans, shells_at, owner, coef, moved, integrals, *refs):
    outs, (shells, table, lam, sig, cols, held, small, sems) = refs[:-8], refs[-8:]
    steps = len(spans)

    def fetch(step):
        here = pl.ds(*spans[step])
        return pltpu.make_async_copy(integrals.at[:, here], held.at[:, here], sems.at[step])

    copy = pltpu.make_async_copy(shells_at, shells, small)
    copy.start()
    for step in range(steps):
        fetch(step).start()

    orbital = lax.broadcasted_iota(jnp.int32, (NOCC, NIJ), 0)
    picks = jnp.concatenate(
        [
            (owner[...] // NOCC == orbital).astype(jnp.bfloat16),
            (owner[...] % NOCC == orbital).astype(jnp.bfloat16),
        ],
        axis=0,
    )
    picks = jnp.dot(picks, moved[...], preferred_element_type=jnp.float32).astype(jnp.bfloat16)

    table[...] = coef[...].astype(jnp.float32).T
    copy.wait()

    for k in range(lam.shape[0] // SHELL):
        here = pl.ds(k * SHELL, SHELL)
        lam[here, :NOCC] = table[pl.ds(pl.multiple_of(shells[0, k] * SHELL, SHELL), SHELL), :]
        sig[here, :NOCC] = table[pl.ds(pl.multiple_of(shells[1, k] * SHELL, SHELL), SHELL), :]
    lam[...] = jnp.dot(
        lam[:, :NOCC].astype(jnp.bfloat16), picks[:NOCC], preferred_element_type=jnp.float32
    )
    sig[...] = jnp.dot(
        sig[:, :NOCC].astype(jnp.bfloat16), picks[NOCC:], preferred_element_type=jnp.float32
    )
    for step in range(steps):
        start, size = spans[step]
        for k in range(start // BLOCK_PAIRS, (start + size) // BLOCK_PAIRS):
            here = pl.ds(k * SHELL, SHELL)
            both = lam[here, :][:, None, :] * sig[here, :][None, :, :]
            cols[pl.ds(k * BLOCK_PAIRS, BLOCK_PAIRS), :] = both.reshape(BLOCK_PAIRS, NIJ).astype(
                jnp.bfloat16
            )
        fetch(step).wait()
        part = lax.dot_general(
            cols[pl.ds(start, size), :], held[:, pl.ds(start, size)], (((0,), (1,)), ((), ())),
            preferred_element_type=jnp.float32,
        )
        at = 0
        for out in outs:
            rows = part[at : at + out.shape[0]]
            out[...] = rows if step == 0 else out[...] + rows
            at += out.shape[0]


def half_rows(integrals, coefficients, ket_shells, pair_owner, pairs, ranges, sizes):
    rows, depth = integrals.shape
    kets = ket_shells.shape[0]
    parts = [jax.ShapeDtypeStruct((size, rows), jnp.float32) for size in sizes * 2]
    ends = [sum(CHUNKS[:at]) * depth // 16 for at in range(len(CHUNKS) + 1)]
    spans = [(start, end - start) for start, end in zip(ends, ends[1:])]
    vmem = pl.BlockSpec(memory_space=pltpu.VMEM)
    hbm = pl.BlockSpec(memory_space=pl.ANY)
    return pl.pallas_call(
        functools.partial(half_rows_kernel, spans),
        out_shape=parts,
        in_specs=[hbm, vmem, vmem, vmem, hbm],
        out_specs=[vmem] * len(parts),
        scratch_shapes=[
            pltpu.SMEM((2, kets), jnp.int32),
            pltpu.VMEM((coefficients.shape[0], NOCC), jnp.float32),
            pltpu.VMEM((kets * SHELL, NIJ), jnp.float32),
            pltpu.VMEM((kets * SHELL, NIJ), jnp.float32),
            pltpu.VMEM((depth, NIJ), jnp.bfloat16),
            pltpu.VMEM((rows, depth), jnp.bfloat16),
            pltpu.SemaphoreType.DMA,
            pltpu.SemaphoreType.DMA((len(spans),)),
        ],
        compiler_params=pltpu.CompilerParams(vmem_limit_bytes=52 * MIB),
    )(ket_shells.T, pair_owner.reshape(1, NIJ), coefficients.T, order_of(pairs, ranges), integrals)


def place_kernel(slots, count, *refs):
    pieces, before = refs[:count], refs[count:-1]
    out = refs[-1]
    rows = out.shape[0]
    for done in before:
        out[...] = done[...]
    upper = lax.broadcasted_iota(jnp.int32, (out.shape[0], LANES), 1) // BLOCK_PAIRS
    for piece in pieces:
        ids = piece[pl.ds(slots // 2 * rows, 1), :].astype(jnp.int32)
        for tile in range(slots // 2):
            value = piece[pl.ds(tile * rows, rows), :]
            turned = pltpu.roll(value, BLOCK_PAIRS, 1)
            for side in range(2):
                block = ids[0, 2 * tile + side]
                there = (jnp.maximum(block, 0) >> 1) * LANES
                pltpu.store(
                    out.at[:, pl.ds(pl.multiple_of(there, LANES), LANES)],
                    jnp.where((block & 1) == side, value, turned),
                    mask=upper == jnp.where(block >= 0, block & 1, 2),
                )


def placed_rows(pieces, before, slots, blocks):
    rows = pieces[0].shape[0] // (slots // 2)
    vmem = pl.BlockSpec(memory_space=pltpu.VMEM)
    return pl.pallas_call(
        functools.partial(place_kernel, slots, len(pieces)),
        out_shape=jax.ShapeDtypeStruct((rows, blocks * BLOCK_PAIRS), jnp.float32),
        in_specs=[vmem] * (len(pieces) + len(before)),
        out_specs=vmem,
        compiler_params=pltpu.CompilerParams(vmem_limit_bytes=8 * MIB),
    )(*pieces, *before)


def sum_kernel(mine, theirs, earlier, lower, upper):
    half = lower.shape[0]
    lower[...] = mine[:half] + theirs[:half]
    upper[...] = mine[half:] + theirs[half:]


def summed(mine, theirs, earlier, cost):
    vmem = pl.BlockSpec(memory_space=pltpu.VMEM)
    half = jax.ShapeDtypeStruct((mine.shape[0] // 2, mine.shape[1]), jnp.float32)
    return pl.pallas_call(
        sum_kernel,
        out_shape=[half] * 2,
        in_specs=[vmem] * 2 + [pl.BlockSpec(memory_space=pl.ANY)],
        out_specs=[vmem] * 2,
        cost_estimate=pl.CostEstimate(flops=cost, bytes_accessed=0, transcendentals=0),
        compiler_params=pltpu.CompilerParams(vmem_limit_bytes=8 * MIB),
    )(mine, theirs, earlier)


def merge_kernel(count, mine, theirs, ids, earlier, *outs):
    tiles = mine.shape[1] // LANES
    rows = mine.shape[0] // count
    for d in range(count):
        here = pl.ds(d * rows, rows)
        for tile in range(tiles):
            lanes = pl.ds(tile * LANES, LANES)
            outs[d][pl.ds(tile * rows, rows), :] = mine[here, lanes] + theirs[here, lanes]
        outs[d][pl.ds(tiles * rows, 1), :] = ids[...]


def merged(mine, theirs, ids, earlier, count, cost):
    vmem = pl.BlockSpec(memory_space=pltpu.VMEM)
    rows = theirs.shape[0] // count
    one = jax.ShapeDtypeStruct((rows * (mine.shape[1] // LANES) + 1, LANES), jnp.float32)
    return pl.pallas_call(
        functools.partial(merge_kernel, count),
        out_shape=[one] * count,
        in_specs=[vmem] * 3 + [pl.BlockSpec(memory_space=pl.ANY)],
        out_specs=[vmem] * count,
        cost_estimate=pl.CostEstimate(flops=cost, bytes_accessed=0, transcendentals=0),
        compiler_params=pltpu.CompilerParams(vmem_limit_bytes=8 * MIB),
    )(mine, theirs, ids, earlier)


def swap(value, axis, size, far):
    return lax.ppermute(value, axis, [(i, i ^ far) for i in range(size)])


def local(pairs, ranges, integrals, coefficients, ket_shells, block_ids, pair_owner):
    slots = block_ids.shape[0]
    each = NIJ // (pairs * ranges)
    some = max(pairs // 4, 1)
    firsts = list(range(0, pairs, some))
    sizes = [some * each * (ranges // 2) for _ in firsts]
    parts = half_rows(integrals, coefficients, ket_shells, pair_owner, pairs, ranges, sizes)
    numbers = jnp.pad(block_ids.astype(jnp.float32), (0, LANES - slots)).reshape(1, LANES)
    step = pairs // 2
    firsts = firsts[step // some :: -1] + firsts[step // some + 1 :]
    firsts = firsts[:2] + firsts[3:] + firsts[2:3]
    groups = []
    for first in firsts:
        at = first // some
        groups.append((first, parts[at], swap(parts[at + len(sizes)], "rng", ranges, 1)))
    halves = []
    earlier = groups[0][2]
    for first, mine, theirs in groups:
        lower, upper = summed(mine, theirs, earlier, 10**6)
        halves.append((first, lower, upper))
        earlier = lower
    pieces = [None] * pairs
    earlier = numbers
    for first, lower, upper in halves:
        for bit in range(1, bits(ranges)):
            other = swap(upper, "rng", ranges, 1 << bit)
            if bit < bits(ranges) - 1:
                lower = lower + other
                lower, upper = jnp.split(lower, 2)
        parts = merged(lower, other, numbers, earlier, some, 2 * 10**9 if first == pairs - some else 5 * 10**8)
        earlier = parts[0]
        for at in range(some):
            d = first + at
            pieces[d] = swap(parts[at], "pair", pairs, d) if d else parts[at]
    blocks = slots * pairs // 2
    early = placed_rows(pieces[:-some], [], slots, blocks)
    return placed_rows(pieces[-some:], [early], slots, blocks)


def solution(mesh):
    placed = (
        P(("grp", "pair"), "rng"),
        P("grp", None),
        P(("grp", "rng"), None),
        P(("grp", "pair")),
        P(),
    )
    return jax.shard_map(
        functools.partial(local, mesh.shape["pair"], mesh.shape["rng"]),
        mesh=mesh,
        in_specs=placed,
        out_specs=P(("grp", "pair", "rng"), None),
        check_vma=False,
    )
```
